32 devices in a mesh: cam: 4 (over x, core), tile: 8 (over z, y).
Axes of the slice: x: 2, y: 2, z: 4, core: 2. Of those that a mesh axis runs over, the one named last changes fastest.
Arguments:
- depth_weights: bfloat16 [128, 16, 64, 128], P(('cam', 'tile')), may hold values from 0.049804688 to 1
- context: bfloat16 [128, 16, 128, 128], P(('cam', 'tile')), may hold values from -1.5 to 1.5
- block_owner: int32 [128, 16, 1], P(('cam', 'tile')), may hold values from 0 to 31; in each aligned block of 64 rows (0 to 63, 64 to 127, ..., all dimensions but the last counted through in order) at most 4 rows name the same one
- block_local: int32 [128, 16], P(('cam', 'tile')), may hold values from 0 to 15
- block_cell: int32 [128, 16, 64], P(('cam', 'tile')), may hold values from 0 to 255
- conv_weight: bfloat16 [4, 3, 3, 128, 128], replicated, may hold values from -0.25 to 0.25
- cotangent: bfloat16 [64, 2048, 128], P('cam', 'tile'), may hold values from -6 to 6
Outputs:
- bev_out: bfloat16 [64, 2048, 128], P('cam', 'tile')
- grad_depth: bfloat16 [128, 16, 64, 128], P(('cam', 'tile'))
- grad_context: bfloat16 [128, 16, 128, 128], P(('cam', 'tile'))
The draws below stay inside these ranges and needn't reach their ends.
Inputs may be any that keep to these rules, and one draw needn't show every extreme that they name: `block_owner`: among the blocks of the cameras of one device (aligned groups of 4 cameras) no owner is named by more than 4 blocks, a bound that some block reaches.
All inputs are finite; a program needn't handle non-finite values.
Results may differ from the reference program's by a relative error of at most 0.02.
Values may be sent and summed in bfloat16 or wider, within the bound.
A program may use at most 128 MiB of HBM per device.

```python
import math
import jax
import jax.numpy as jnp
import numpy as np

C = 128
DB = 64
PIX = 128
BLK = 16
TS = 16
TC_DEV = 16
TR_DEV = 1
CAM_DEV = 4
LAYERS = 4
OWNERS = 32
CAMS = 128
GX = 64
GY = 2048
TILES_DEV = 16
CAP = 4
N_TILE = 8


def plant(drawn, key, smallest, high):
    shape = drawn.shape
    spot = [jax.random.randint(jax.random.fold_in(key, axis), (), 0, shape[axis]) for axis in range(len(shape))]
    drawn = drawn.at[tuple(spot)].set(smallest)
    longest = shape.index(max(shape))
    spot[longest] = (spot[longest] + 1) % shape[longest]
    return drawn.at[tuple(spot)].set(high)


def steps_of(rng, shape, pieces, smallest, high):
    def one(dim, blocks):
        heights = jax.random.uniform(jax.random.fold_in(jax.random.fold_in(rng, 6), dim), (blocks,), jnp.float32, smallest / len(pieces), high / len(pieces))
        return jnp.repeat(jnp.exp(heights), shape[dim] // blocks).reshape((-1,) + (1,) * (len(shape) - dim - 1))

    gain = one(*pieces[0])
    for cut in pieces[1:]:
        gain = gain * one(*cut)
    return gain


def routed_block(key, own, number, rows, amount, top, bound, slope):
    order = jax.random.permutation(key, amount)
    packed, ordinary = shares(amount, rows * top, bound, slope, True), shares(amount, rows * top, bound, slope, False)
    places = jnp.arange(amount)

    def named(lengths, offset_by):
        used = int((lengths > 0).sum())
        fixed = max(1, used // 4)
        shifted = fixed + (places - fixed + offset_by * (used - fixed)) % max(1, amount - fixed)
        return jnp.zeros((amount,), jnp.int32).at[order[jnp.where(places < fixed, places, shifted)]].set(jnp.asarray(lengths, jnp.int32))

    lengths = jnp.where(number % 4 == 0, named(packed, number // 4), named(ordinary, number - number // 4 - 1))
    mixed = jax.random.permutation(jax.random.fold_in(own, 3), amount)
    donor, receiver = mixed[0:amount // 2 * 2:2], mixed[1:amount // 2 * 2:2]
    room = jnp.minimum(lengths[donor] - 1, bound - lengths[receiver]) // 2
    room = jnp.where((donor == order[0]) | (receiver == order[0]) | (lengths[receiver] == 0), 0, jnp.maximum(room, 0))
    shifted = jax.random.randint(jax.random.fold_in(own, 4), (amount // 2,), 0, 1 << 20) % (room + 1)
    lengths = lengths.at[donor].add(-shifted).at[receiver].add(shifted)
    labels = jnp.searchsorted(jnp.cumsum(lengths), jnp.arange(rows * top), side="right").astype(jnp.int32)
    grid = labels.reshape(top, rows).T
    grid = grid[jax.random.permutation(jax.random.fold_in(own, 1), rows)]
    offset_by = jax.random.randint(jax.random.fold_in(own, 2), (rows, 1), 0, top)
    return jnp.take_along_axis(grid, (jnp.arange(top)[None, :] + offset_by) % top, axis=1)


def shares(count, total, bound, slope, full):
    weights = [(1 << 20) // math.isqrt(rank ** slope) + 1 for rank in range(1, count + 1)]
    largest = bound if full else min(bound, max(-(-total // count), total * weights[0] // sum(weights)))
    least = 1 if total - largest >= count - 1 else 0
    counts, rest = [largest] + [least] * (count - 1), total - largest - least * (count - 1)
    while rest > 0:
        movable = [i for i in range(1, count) if counts[i] < largest] or [i for i in range(1, count) if counts[i] < bound]
        whole, remaining = sum([weights[i] for i in movable]), rest
        for i in movable:
            more = min(bound - counts[i], max(1, remaining * weights[i] // whole), rest)
            counts[i] = counts[i] + more
            rest = rest - more
    return np.array(counts)


def gaussian(stream_key, shape, deviation, reach, cuts=(), kind=jnp.bfloat16):
    loudness = steps_of(stream_key, shape, cuts, -0.22, 0.18) if cuts else 1.0
    array = jax.random.normal(stream_key, shape, jnp.float32) * deviation * loudness
    return jnp.minimum(jnp.maximum(array, -reach), reach).astype(kind)


def setup_inputs(seed: int = 0) -> dict:
    key_list = jax.random.split(jax.random.key(seed), 8)
    depth_weights = jnp.clip(jnp.exp(math.log(1.0) - 2.9996462 * jax.random.uniform(key_list[0], (CAMS, BLK, DB, PIX), jnp.float32) ** steps_of(key_list[0], (CAMS, BLK, DB, PIX), ((0, 32),), -0.2, 0.2)), 0.049804688, 1.0).astype(jnp.bfloat16)
    context = gaussian(key_list[1], (CAMS, BLK, PIX, C), 0.25, 1.5, ((0, 32),))
    block_owner_keys = jax.random.split(jax.random.fold_in(key_list[2], 1), CAMS * BLK // (CAM_DEV * BLK))
    block_owner_turns = jax.random.permutation(jax.random.fold_in(key_list[2], 3), CAMS * BLK // (CAM_DEV * BLK))
    block_owner = jax.vmap(lambda own, number: routed_block(jax.random.fold_in(key_list[2], 2), own, number, CAM_DEV * BLK, OWNERS, 1, CAP, 2))(block_owner_keys, block_owner_turns).reshape((CAMS, BLK, 1))
    block_local = plant(jax.random.randint(key_list[3], (CAMS, BLK), 0, TILES_DEV), jax.random.fold_in(key_list[3], 1), 0, TILES_DEV - 1).astype(jnp.int32)
    block_cell = plant(jax.random.randint(key_list[4], (CAMS, BLK, DB), 0, TS * TS), jax.random.fold_in(key_list[4], 1), 0, (TS * TS) - 1).astype(jnp.int32)
    conv_weight = gaussian(key_list[5], (LAYERS, 3, 3, C, C), (4 * C) ** -0.5, 0.25)
    cotangent = gaussian(key_list[6], (GX, GY, C), 1.0, 6.0, ((0, 4), (1, 8)))
    return {"depth_weights": depth_weights, "context": context, "block_owner": block_owner, "block_local": block_local, "block_cell": block_cell, "conv_weight": conv_weight, "cotangent": cotangent}


def silu_slope(preact):
    sigma = jax.nn.sigmoid(preact)
    return sigma * (1.0 + preact * (1.0 - sigma))


def conv_taps(padded, kernel, flipped):
    rows_out = padded.shape[0] - 2
    cols_out = padded.shape[1] - 2
    total = jnp.zeros((rows_out, cols_out, kernel.shape[3]), jnp.float32)
    for row_tap in range(3):
        for col_tap in range(3):
            window = padded[row_tap:row_tap + rows_out, col_tap:col_tap + cols_out].astype(jnp.float32)
            if flipped:
                total = total + jnp.einsum("xyo,io->xyi", window, kernel[2 - row_tap, 2 - col_tap].astype(jnp.float32))
            else:
                total = total + jnp.einsum("xyi,io->xyo", window, kernel[row_tap, col_tap].astype(jnp.float32))
    return total


def pad_grid(field):
    return jnp.pad(field, ((1, 1), (1, 1), (0, 0)))


def reference(depth_weights, context, block_owner, block_local, block_cell, conv_weight, cotangent):
    grid_rows = cotangent.shape[0]
    grid_cols = cotangent.shape[1]
    channels = context.shape[3]
    depth_wide = depth_weights.astype(jnp.float32)
    context_wide = context.astype(jnp.float32)
    lifted = jnp.einsum("nbdp,nbpc->nbdc", depth_wide, context_wide).astype(jnp.bfloat16)
    owner_ids = block_owner[..., 0]
    region_rows = TR_DEV * TS
    region_cols = TC_DEV * TS
    row_base = (owner_ids // N_TILE) * region_rows + (block_local // TC_DEV) * TS
    col_base = (owner_ids % N_TILE) * region_cols + (block_local % TC_DEV) * TS
    cell_row = row_base[..., None] + block_cell // TS
    cell_col = col_base[..., None] + block_cell % TS
    cell_index = (cell_row * grid_cols + cell_col).astype(jnp.int32)
    splat_sum = jax.ops.segment_sum(lifted.reshape(-1, channels).astype(jnp.float32), cell_index.reshape(-1), num_segments=grid_rows * grid_cols)
    activation = splat_sum.reshape(grid_rows, grid_cols, channels).astype(jnp.bfloat16)
    stored = []
    for layer in range(LAYERS):
        preact = conv_taps(pad_grid(activation), conv_weight[layer], False)
        stored.append(preact)
        activation = jax.nn.silu(preact).astype(jnp.bfloat16)
    bev_out = activation
    gradient = cotangent
    for layer in range(LAYERS - 1, -1, -1):
        grad_pre = (gradient.astype(jnp.float32) * silu_slope(stored[layer])).astype(jnp.bfloat16)
        gradient = conv_taps(pad_grid(grad_pre), conv_weight[layer], True).astype(jnp.bfloat16)
    back_rows = gradient.reshape(grid_rows * grid_cols, channels)[cell_index]
    back_wide = back_rows.astype(jnp.float32)
    grad_depth = jnp.einsum("nbdc,nbpc->nbdp", back_wide, context_wide).astype(jnp.bfloat16)
    grad_context = jnp.einsum("nbdp,nbdc->nbpc", depth_wide, back_wide).astype(jnp.bfloat16)
    return (bev_out, grad_depth, grad_context)
```

```python
import functools

import jax
import jax.numpy as jnp
from jax import lax
from jax.experimental import pallas as pl
from jax.experimental.pallas import tpu as pltpu
from jax.sharding import PartitionSpec as P

TS = 16
LAYERS = 4
ROW_HALO = 2 * LAYERS
COL_HALO = 16
META_ROWS = 16
MESH = pl.DeviceIdType.MESH
BF = jnp.bfloat16
F32 = jnp.float32
DIRECTIONS = [(dx, dy) for dx in (-1, 0, 1) for dy in (-1, 0, 1) if (dx, dy) != (0, 0)]


def lift_kernel(cap, bins, owner_ref, meta_ref, depth_ref, context_ref, send_ref, count, meta_rows):
    step = pl.program_id(0)
    owners = send_ref.shape[0]
    blocks = depth_ref.shape[0]

    @pl.when(step == 0)
    def _():
        meta_rows[...] = jnp.zeros_like(meta_rows)

        def clear(o, carry):
            count[o] = 0
            return carry

        lax.fori_loop(0, owners, clear, 0)

    for b in range(blocks):
        owner = owner_ref[step * blocks + b]
        rank = count[owner]
        count[owner] = rank + 1
        lifted = jnp.dot(depth_ref[b], context_ref[b], preferred_element_type=F32).astype(BF)
        send_ref[owner, pl.ds(pl.multiple_of(rank * bins, bins), bins), :] = lifted
        meta_rows[owner, pl.ds(rank, 1), :] = meta_ref[pl.ds(b, 1), :]

    @pl.when(step == pl.num_programs(0) - 1)
    def _():
        def put(o, carry):
            rows = meta_rows[o]
            send_ref[o, cap * bins : cap * bins + META_ROWS, :] = jnp.concatenate(
                [rows, jnp.zeros_like(rows)], axis=0
            ).astype(BF)
            return carry

        lax.fori_loop(0, owners, put, 0)


def lift(depth, context, owner, meta, owners, cap):
    blocks, bins, pixels = depth.shape
    channels = context.shape[2]
    chunk = 16
    rows = cap * bins + META_ROWS
    return pl.pallas_call(
        functools.partial(lift_kernel, cap, bins),
        grid=(blocks // chunk,),
        out_shape=jax.ShapeDtypeStruct((owners, rows, channels), BF),
        in_specs=[
            pl.BlockSpec(memory_space=pltpu.SMEM),
            pl.BlockSpec((chunk, 128), lambda i: (i, 0)),
            pl.BlockSpec((chunk, bins, pixels), lambda i: (i, 0, 0)),
            pl.BlockSpec((chunk, pixels, channels), lambda i: (i, 0, 0)),
        ],
        out_specs=pl.BlockSpec((owners, rows, channels), lambda i: (0, 0, 0)),
        scratch_shapes=[pltpu.SMEM((owners,), jnp.int32), pltpu.VMEM((owners, 8, 128), F32)],
        compiler_params=pltpu.CompilerParams(vmem_limit_bytes=40 << 20),
        name="lift",
    )(owner, meta, depth, context)


def splat_kernel(cap, bins, tile_ref, valid_ref, recv_ref, out_ref, sums):
    owners = recv_ref.shape[0]
    tiles = sums.shape[0]
    cells = TS * TS
    sums[...] = jnp.zeros_like(sums)

    def source(o, carry):
        def pair(first):
            meta = recv_ref[o, cap * bins : cap * bins + META_ROWS, :].astype(F32)
            parts = []
            for k in (first, first + 1):
                row = meta[k : k + 1, 0:bins]
                live = meta[k : k + 1, bins + 1 : bins + 2] > 0.5
                place = jnp.where(live, row, -1.0)
                wide = jnp.broadcast_to(place, (cells, bins))
                index = lax.broadcasted_iota(jnp.int32, (cells, bins), 0).astype(F32)
                hot = jnp.where(wide == index, 1.0, 0.0).astype(BF)
                rows = recv_ref[o, k * bins : (k + 1) * bins, :]
                rows = jnp.where(jnp.broadcast_to(live, rows.shape), rows.astype(F32), 0.0).astype(BF)
                parts.append(jnp.dot(hot, rows, preferred_element_type=F32))
            for k, part in zip((first, first + 1), parts):
                tile = tile_ref[o * cap + k]
                sums[tile] = sums[tile] + part

        for first in range(0, cap, 2):
            @pl.when(valid_ref[o * cap + first] > 0)
            def _():
                pair(first)

        return carry

    lax.fori_loop(0, owners, source, 0)
    for tile in range(tiles):
        for row in range(TS):
            out_ref[row, tile * TS : (tile + 1) * TS, :] = sums[
                tile, row * TS : (row + 1) * TS, :
            ].astype(BF)


def splat(received, slot_tile, slot_valid, cap, bins, rows, cols):
    channels = received.shape[2]
    tiles = (rows // TS) * (cols // TS)
    return pl.pallas_call(
        functools.partial(splat_kernel, cap, bins),
        out_shape=jax.ShapeDtypeStruct((rows, cols, channels), BF),
        in_specs=[
            pl.BlockSpec(memory_space=pltpu.SMEM),
            pl.BlockSpec(memory_space=pltpu.SMEM),
            pl.BlockSpec(memory_space=pltpu.VMEM),
        ],
        out_specs=pl.BlockSpec(memory_space=pltpu.VMEM),
        scratch_shapes=[pltpu.VMEM((tiles, TS * TS, channels), F32)],
        compiler_params=pltpu.CompilerParams(vmem_limit_bytes=40 << 20),
        name="splat",
    )(slot_tile, slot_valid, received)


def halo_kernel(cams, tiles, h_ref, g_ref, hp_ref, gp_ref, send_sem, recv_sem, local_sem):
    cam = lax.axis_index("cam")
    tile = lax.axis_index("tile")
    rows, cols = h_ref.shape[0], h_ref.shape[1]

    def there(dx, dy):
        ok = None
        for at, step, count in ((cam, dx, cams), (tile, dy, tiles)):
            if step:
                here = (at + step >= 0) & (at + step < count)
                ok = here if ok is None else ok & here
        return ok

    barrier = pltpu.get_barrier_semaphore()
    arrivals = 0
    for dx, dy in DIRECTIONS:
        near = there(dx, dy)
        arrivals = arrivals + near.astype(jnp.int32)

        @pl.when(near)
        def _():
            pl.semaphore_signal(
                barrier, inc=1, device_id=(cam + dx, tile + dy), device_id_type=MESH
            )

    pl.semaphore_wait(barrier, arrivals)

    def copies(index):
        dx, dy = DIRECTIONS[index]
        made = []
        for which, (source, target, halo) in enumerate(
            ((h_ref, hp_ref, ROW_HALO), (g_ref, gp_ref, LAYERS))
        ):
            row_src, row_dst, row_len = {
                -1: (0, halo + rows, halo),
                0: (0, halo, rows),
                1: (rows - halo, 0, halo),
            }[dx]
            col_src, col_dst, col_len = {
                -1: (0, COL_HALO + cols, COL_HALO),
                0: (0, COL_HALO, cols),
                1: (cols - COL_HALO, 0, COL_HALO),
            }[dy]
            made.append(
                pltpu.make_async_remote_copy(
                    src_ref=source.at[pl.ds(row_src, row_len), pl.ds(col_src, col_len)],
                    dst_ref=target.at[pl.ds(row_dst, row_len), pl.ds(col_dst, col_len)],
                    send_sem=send_sem.at[2 * index + which],
                    recv_sem=recv_sem.at[2 * index + which],
                    device_id=(cam + dx, tile + dy),
                    device_id_type=MESH,
                )
            )
        return made

    for index in range(len(DIRECTIONS)):
        @pl.when(there(*DIRECTIONS[index]))
        def _():
            for copy in copies(index):
                copy.start()

    own = [
        pltpu.make_async_copy(
            source, target.at[pl.ds(halo, rows), pl.ds(COL_HALO, cols)], local_sem.at[which]
        )
        for which, (source, target, halo) in enumerate(
            ((h_ref, hp_ref, ROW_HALO), (g_ref, gp_ref, LAYERS))
        )
    ]
    for copy in own:
        copy.start()
    for index, (dx, dy) in enumerate(DIRECTIONS):
        @pl.when(there(dx, dy))
        def _():
            for copy in copies(index):
                copy.wait_send()

        @pl.when(there(-dx, -dy))
        def _():
            for copy in copies(index):
                copy.wait_recv()
    for copy in own:
        copy.wait()


def halo_exchange(cells, cotangent, cams, tiles):
    rows, cols, channels = cells.shape
    wide = cols + 2 * COL_HALO
    anywhere = pl.BlockSpec(memory_space=pl.ANY)
    return pl.pallas_call(
        functools.partial(halo_kernel, cams, tiles),
        out_shape=[
            jax.ShapeDtypeStruct((rows + 2 * ROW_HALO, wide, channels), BF),
            jax.ShapeDtypeStruct((rows + 2 * LAYERS, wide, channels), BF),
        ],
        in_specs=[anywhere] * 2,
        out_specs=[anywhere] * 2,
        scratch_shapes=[
            pltpu.SemaphoreType.DMA((2 * len(DIRECTIONS),)),
            pltpu.SemaphoreType.DMA((2 * len(DIRECTIONS),)),
            pltpu.SemaphoreType.DMA((2,)),
        ],
        compiler_params=pltpu.CompilerParams(collective_id=0, has_side_effects=True),
        name="halo",
    )(cells, cotangent)


def conv_kernel(
    cap, bins, grid_rows, grid_cols,
    tile_ref, valid_ref, hp_ref, gp_ref, weight_ref, cells_ref,
    out_ref, back_ref,
    fields, slopes, masks, wide_weight, grads,
):
    rows, cols = out_ref.shape[0], out_ref.shape[1]
    channels = out_ref.shape[2]
    width = hp_ref.shape[1]
    tall = hp_ref.shape[0]
    row_first = lax.axis_index("cam") * rows - ROW_HALO
    col_first = lax.axis_index("tile") * cols - COL_HALO
    column = lax.broadcasted_iota(jnp.int32, (width, channels), 0) + col_first
    masks[0] = jnp.zeros((width, channels), F32)
    masks[1] = jnp.where((column >= 0) & (column < grid_cols), 1.0, 0.0)
    wide_weight[...] = jnp.zeros_like(wide_weight)

    def mask_of(row):
        at = row + row_first
        return masks[((at >= 0) & (at < grid_rows)).astype(jnp.int32)]

    def clean(row, carry):
        fields[0, row] = jnp.where(mask_of(row) > 0.5, hp_ref[row].astype(F32), 0.0).astype(BF)
        return carry

    lax.fori_loop(0, tall, clean, 0)

    def spread(index):
        slot = index % 2
        for j in range(2):
            for s in range(3):
                for r in range(3):
                    k = r + j
                    wide_weight[
                        slot,
                        k * channels : (k + 1) * channels,
                        (j * 3 + s) * channels : (j * 3 + s + 1) * channels,
                    ] = weight_ref[index, r, s]

    def sweep(index, source, first, last, finish):
        spread(index)

        def one(row):
            window = jnp.concatenate([fields[source, row - 1 + k] for k in range(4)], axis=1)
            taps = jnp.dot(window, wide_weight[index % 2], preferred_element_type=F32)
            for j in range(2):
                base = j * 3 * channels
                left = taps[:, base : base + channels]
                middle = taps[:, base + channels : base + 2 * channels]
                right = taps[:, base + 2 * channels : base + 3 * channels]
                finish(
                    row + j,
                    pltpu.roll(left, 1, 0) + middle + pltpu.roll(right, width - 1, 0),
                )

        pairs = (last - first) // 2

        def two(step, carry):
            one(first + 4 * step)
            one(first + 4 * step + 2)
            return carry

        lax.fori_loop(0, pairs // 2, two, 0)
        if pairs % 2:
            one(last - 2)

    for layer in range(1, LAYERS + 1):
        def finish_forward(row, pre, layer=layer):
            sigma = 0.5 * jnp.tanh(0.5 * pre) + 0.5
            value = pre * sigma
            slope = sigma * (1.0 + pre * (1.0 - sigma))
            if layer < LAYERS:
                slopes[layer - 1, row] = slope
                fields[layer % 2, row] = (value * mask_of(row)).astype(BF)
            else:
                grad = gp_ref[row - LAYERS].astype(F32)
                grad = jnp.where(mask_of(row) > 0.5, grad, 0.0)
                fields[layer % 2, row] = (grad * slope).astype(BF)
                inner = jnp.clip(row - ROW_HALO, 0, rows - 1)

                @pl.when(inner == row - ROW_HALO)
                def _():
                    out_ref[inner] = value[COL_HALO : COL_HALO + cols].astype(BF)

        sweep(layer - 1, (layer - 1) % 2, layer, tall - layer, finish_forward)

    for layer in range(LAYERS, 0, -1):
        done = LAYERS - layer

        def finish_backward(row, grad, layer=layer, done=done):
            grad = grad.astype(BF)
            if layer > 1:
                fields[(done + 1) % 2, row] = (
                    grad.astype(F32) * slopes[layer - 2, row] * mask_of(row)
                ).astype(BF)
            else:
                inner = row - ROW_HALO
                for t in range(cols // TS):
                    grads[t, pl.ds(pl.multiple_of(inner * TS, TS), TS), :] = grad[
                        COL_HALO + t * TS : COL_HALO + (t + 1) * TS
                    ]

        sweep(
            LAYERS + layer - 1, done % 2,
            ROW_HALO + 1 - layer, ROW_HALO + rows - 1 + layer, finish_backward,
        )

    slots = cells_ref.shape[1]
    owners = slots // cap
    lane = lax.broadcasted_iota(jnp.int32, (bins, slots), 1)
    cell = lax.broadcasted_iota(jnp.int32, (bins, TS * TS), 1).astype(F32)

    def send_back(o, carry):
        def pair(first):
            for k in (first, first + 1):
                slot = o * cap + k
                place = jnp.sum(jnp.where(lane == slot, cells_ref[...], 0.0), axis=1, keepdims=True)
                hot = jnp.where(place == cell, 1.0, 0.0).astype(BF)
                back_ref[pl.ds(pl.multiple_of(slot * bins, bins), bins), :] = jnp.dot(
                    hot, grads[tile_ref[slot]], preferred_element_type=F32
                ).astype(BF)

        for first in range(0, cap, 2):
            @pl.when(valid_ref[o * cap + first] > 0)
            def _():
                pair(first)

        return carry

    lax.fori_loop(0, owners, send_back, 0)


def convolve(hp, gp, weights, slot_tile, slot_valid, cells, cap, bins, rows, cols, grid_shape):
    tall, wide, channels = hp.shape
    assert rows == TS
    vmem = pl.BlockSpec(memory_space=pltpu.VMEM)
    smem = pl.BlockSpec(memory_space=pltpu.SMEM)
    return pl.pallas_call(
        functools.partial(conv_kernel, cap, bins, *grid_shape),
        out_shape=[
            jax.ShapeDtypeStruct((rows, cols, channels), BF),
            jax.ShapeDtypeStruct((cells.shape[1] * bins, channels), BF),
        ],
        in_specs=[smem, smem, vmem, vmem, vmem, vmem],
        out_specs=[vmem, vmem],
        scratch_shapes=[
            pltpu.VMEM((2, tall, wide, channels), BF),
            pltpu.VMEM((LAYERS - 1, tall, wide, channels), F32),
            pltpu.VMEM((2, wide, channels), F32),
            pltpu.VMEM((2, 4 * channels, 6 * channels), BF),
            pltpu.VMEM((cols // TS, TS * TS, channels), BF),
        ],
        compiler_params=pltpu.CompilerParams(vmem_limit_bytes=56 << 20),
        name="convolutions",
    )(slot_tile, slot_valid, hp, gp, weights, cells)


def per_device(
    depth_weights, context, block_owner, block_local, block_cell, conv_weight, cotangent
):
    cams_here, blocks_cam, bins, pixels = depth_weights.shape
    channels = context.shape[3]
    rows, cols = cotangent.shape[0], cotangent.shape[1]
    cams = lax.axis_size("cam")
    tiles = lax.axis_size("tile")
    owners = cams * tiles
    blocks = cams_here * blocks_cam
    cap = max(2, 2 * blocks // owners)
    depth = depth_weights.reshape(blocks, bins, pixels)
    flat_context = context.reshape(blocks, pixels, channels)
    owner = block_owner.reshape(blocks)
    meta = jnp.concatenate(
        [
            block_cell.reshape(blocks, bins),
            block_local.reshape(blocks, 1),
            jnp.ones((blocks, 1), jnp.int32),
            jnp.zeros((blocks, 128 - bins - 2), jnp.int32),
        ],
        axis=1,
    ).astype(F32)
    sent = lift(depth, flat_context, owner, meta, owners, cap)
    received = lax.all_to_all(sent, ("cam", "tile"), split_axis=0, concat_axis=0, tiled=True)
    slot_meta = received[:, cap * bins : cap * bins + cap, :].reshape(owners * cap, 128)
    slot_tile = slot_meta[:, bins].astype(jnp.int32)
    slot_valid = slot_meta[:, bins + 1].astype(jnp.int32)
    slot_cells = slot_meta[:, :bins].astype(F32).T
    backward = jnp.swapaxes(conv_weight[:, ::-1, ::-1], 3, 4)
    weights = jnp.concatenate([conv_weight, backward], axis=0)
    cells = splat(received, slot_tile, slot_valid, cap, bins, rows, cols)
    hp, gp = halo_exchange(cells, cotangent, cams, tiles)
    bev_out, back = convolve(
        hp, gp, weights, slot_tile, slot_valid, slot_cells, cap, bins, rows, cols,
        (rows * cams, cols * tiles),
    )
    returned = lax.all_to_all(
        back.reshape(owners, cap * bins, channels),
        ("cam", "tile"), split_axis=0, concat_axis=0, tiled=True,
    ).reshape(owners * cap, bins, channels)
    positions = jnp.arange(blocks, dtype=jnp.int32)
    earlier = (owner[:, None] == owner[None, :]) & (positions[None, :] < positions[:, None])
    slot_index = owner * cap + jnp.sum(earlier.astype(jnp.int32), axis=1)
    block_grad = returned[slot_index]
    grad_context = jnp.einsum(
        "bdp,bdc->bpc", depth, block_grad, preferred_element_type=F32
    ).astype(BF)
    grad_depth = jnp.einsum(
        "bdc,bpc->bdp", block_grad, flat_context, preferred_element_type=F32
    ).astype(BF)
    return (
        bev_out,
        grad_depth.reshape(depth_weights.shape),
        grad_context.reshape(context.shape),
    )


def solution(mesh):
    placed = (
        P(("cam", "tile"), None, None, None),
        P(("cam", "tile"), None, None, None),
        P(("cam", "tile"), None, None),
        P(("cam", "tile"), None),
        P(("cam", "tile"), None, None),
        P(),
        P("cam", "tile", None),
    )
    return jax.shard_map(
        per_device,
        mesh=mesh,
        in_specs=placed,
        out_specs=(
            P("cam", "tile", None),
            P(("cam", "tile"), None, None, None),
            P(("cam", "tile"), None, None, None),
        ),
        check_vma=False,
    )
```

```python
import functools

import jax
import jax.numpy as jnp
from jax import lax
from jax.experimental import pallas as pl
from jax.experimental.pallas import tpu as pltpu
from jax.sharding import PartitionSpec as P

TS = 16
LAYERS = 4
ROW_HALO = 2 * LAYERS
COL_HALO = 16
META_ROWS = 16
GROUP = 4
MESH = pl.DeviceIdType.MESH
BF = jnp.bfloat16
F32 = jnp.float32
DIRECTIONS = [(dx, dy) for dx in (-1, 0, 1) for dy in (-1, 0, 1) if (dx, dy) != (0, 0)]


def lift_kernel(cap, bins, owner_ref, meta_ref, depth_ref, context_ref, send_ref, count, meta_rows):
    step = pl.program_id(0)
    owners = send_ref.shape[0]
    blocks = depth_ref.shape[0]

    @pl.when(step == 0)
    def _():
        meta_rows[...] = jnp.zeros_like(meta_rows)

        def clear(o, carry):
            count[o] = 0
            return carry

        lax.fori_loop(0, owners, clear, 0)

    for b in range(blocks):
        owner = owner_ref[step * blocks + b]
        rank = count[owner]
        count[owner] = rank + 1
        lifted = jnp.dot(depth_ref[b], context_ref[b], preferred_element_type=F32).astype(BF)
        send_ref[owner, pl.ds(pl.multiple_of(rank * bins, bins), bins), :] = lifted
        meta_rows[owner, pl.ds(rank, 1), :] = meta_ref[pl.ds(b, 1), :]

    @pl.when(step == pl.num_programs(0) - 1)
    def _():
        def put(o, carry):
            rows = meta_rows[o]
            send_ref[o, cap * bins : cap * bins + META_ROWS, :] = jnp.concatenate(
                [rows, jnp.zeros_like(rows)], axis=0
            ).astype(BF)
            return carry

        lax.fori_loop(0, owners, put, 0)


def lift(depth, context, owner, meta, owners, cap):
    blocks, bins, pixels = depth.shape
    channels = context.shape[2]
    chunk = 16
    rows = cap * bins + META_ROWS
    return pl.pallas_call(
        functools.partial(lift_kernel, cap, bins),
        grid=(blocks // chunk,),
        out_shape=jax.ShapeDtypeStruct((owners, rows, channels), BF),
        in_specs=[
            pl.BlockSpec(memory_space=pltpu.SMEM),
            pl.BlockSpec((chunk, 128), lambda i: (i, 0)),
            pl.BlockSpec((chunk, bins, pixels), lambda i: (i, 0, 0)),
            pl.BlockSpec((chunk, pixels, channels), lambda i: (i, 0, 0)),
        ],
        out_specs=pl.BlockSpec((owners, rows, channels), lambda i: (0, 0, 0)),
        scratch_shapes=[pltpu.SMEM((owners,), jnp.int32), pltpu.VMEM((owners, 8, 128), F32)],
        compiler_params=pltpu.CompilerParams(vmem_limit_bytes=40 << 20),
        name="lift",
    )(owner, meta, depth, context)


def list_slots(valid_ref, chosen):
    def look(slot, count):
        chosen[count] = slot
        return count + valid_ref[slot]

    return lax.fori_loop(0, valid_ref.shape[0], look, 0)


def splat_kernel(cap, bins, tile_ref, valid_ref, meta_ref, recv_ref, out_ref, sums, chosen):
    tiles = sums.shape[0]
    cells = TS * TS
    sums[...] = jnp.zeros_like(sums)
    live_slots = list_slots(valid_ref, chosen)

    def group(step, carry):
        parts = []
        for k in range(GROUP):
            at = step * GROUP + k
            slot = chosen[jnp.minimum(at, live_slots - 1)]
            row = meta_ref[pl.ds(slot, 1), :][:, 0:bins]
            place = jnp.where(at < live_slots, row, -1.0)
            wide = jnp.broadcast_to(place, (cells, bins))
            index = lax.broadcasted_iota(jnp.int32, (cells, bins), 0).astype(F32)
            hot = jnp.where(wide == index, 1.0, 0.0).astype(BF)
            start = pl.multiple_of(slot % cap * bins, bins)
            rows = recv_ref[slot // cap, pl.ds(start, bins), :]
            parts.append((tile_ref[slot], jnp.dot(hot, rows, preferred_element_type=F32)))
        for tile, part in parts:
            sums[tile] = sums[tile] + part
        return carry

    lax.fori_loop(0, (live_slots + GROUP - 1) // GROUP, group, 0)
    for tile in range(tiles):
        for row in range(TS):
            out_ref[row, tile * TS : (tile + 1) * TS, :] = sums[
                tile, row * TS : (row + 1) * TS, :
            ].astype(BF)


def splat(received, slot_tile, slot_valid, slot_meta, cap, bins, rows, cols):
    channels = received.shape[2]
    tiles = (rows // TS) * (cols // TS)
    vmem = pl.BlockSpec(memory_space=pltpu.VMEM)
    smem = pl.BlockSpec(memory_space=pltpu.SMEM)
    return pl.pallas_call(
        functools.partial(splat_kernel, cap, bins),
        out_shape=jax.ShapeDtypeStruct((rows, cols, channels), BF),
        in_specs=[smem, smem, vmem, vmem],
        out_specs=vmem,
        scratch_shapes=[
            pltpu.VMEM((tiles, TS * TS, channels), F32),
            pltpu.SMEM((slot_valid.shape[0] + 1,), jnp.int32),
        ],
        compiler_params=pltpu.CompilerParams(vmem_limit_bytes=40 << 20),
        name="splat",
    )(slot_tile, slot_valid, slot_meta, received)


def halo_kernel(
    cams, tiles, h_ref, g_ref,
    h_ns, h_ew, h_corner, g_ns, g_ew, g_corner,
    h_edge, g_edge, send_sem, recv_sem,
):
    cam = lax.axis_index("cam")
    tile = lax.axis_index("tile")
    rows, cols = h_ref.shape[0], h_ref.shape[1]

    def there(dx, dy):
        ok = None
        for at, step, count in ((cam, dx, cams), (tile, dy, tiles)):
            if step:
                here = (at + step >= 0) & (at + step < count)
                ok = here if ok is None else ok & here
        return ok

    barrier = pltpu.get_barrier_semaphore()
    arrivals = 0
    for dx, dy in DIRECTIONS:
        near = there(dx, dy)
        arrivals = arrivals + near.astype(jnp.int32)

        @pl.when(near)
        def _():
            pl.semaphore_signal(
                barrier, inc=1, device_id=(cam + dx, tile + dy), device_id_type=MESH
            )

    for edge, field in ((h_edge, h_ref), (g_edge, g_ref)):
        edge[0] = field[:, 0:COL_HALO, :]
        edge[1] = field[:, cols - COL_HALO : cols, :]
    pl.semaphore_wait(barrier, arrivals)

    def copies(index):
        dx, dy = DIRECTIONS[index]
        side_row, side_col = (0 if dx == 1 else 1), (0 if dy == 1 else 1)
        own_col = 0 if dy == -1 else 1
        pairs = []
        for field, edge, ns, ew, corner, halo in (
            (h_ref, h_edge, h_ns, h_ew, h_corner, ROW_HALO),
            (g_ref, g_edge, g_ns, g_ew, g_corner, LAYERS),
        ):
            first = 0 if dx == -1 else rows - halo
            if dy == 0:
                for part in range(0, halo, LAYERS):
                    pairs.append(
                        (
                            field.at[pl.ds(first + part, LAYERS)],
                            ns.at[side_row, pl.ds(part, LAYERS)],
                        )
                    )
            elif dx == 0:
                pairs.append((edge.at[own_col], ew.at[side_col]))
            else:
                pairs.append(
                    (edge.at[own_col, pl.ds(first, halo)], corner.at[2 * side_row + side_col])
                )
        return [
            pltpu.make_async_remote_copy(
                src_ref=source,
                dst_ref=target,
                send_sem=send_sem.at[3 * index + which],
                recv_sem=recv_sem.at[3 * index + which],
                device_id=(cam + dx, tile + dy),
                device_id_type=MESH,
            )
            for which, (source, target) in enumerate(pairs)
        ]

    for index in range(len(DIRECTIONS)):
        @pl.when(there(*DIRECTIONS[index]))
        def _():
            for copy in copies(index):
                copy.start()

    for index, (dx, dy) in enumerate(DIRECTIONS):
        @pl.when(there(dx, dy))
        def _():
            for copy in copies(index):
                copy.wait_send()

        @pl.when(there(-dx, -dy))
        def _():
            for copy in copies(index):
                copy.wait_recv()


def halo_exchange(cells, cotangent, cams, tiles):
    rows, cols, channels = cells.shape
    vmem = pl.BlockSpec(memory_space=pltpu.VMEM)

    def parts(halo):
        return [
            jax.ShapeDtypeStruct((2, halo, cols, channels), BF),
            jax.ShapeDtypeStruct((2, rows, COL_HALO, channels), BF),
            jax.ShapeDtypeStruct((4, halo, COL_HALO, channels), BF),
        ]

    return pl.pallas_call(
        functools.partial(halo_kernel, cams, tiles),
        out_shape=parts(ROW_HALO) + parts(LAYERS),
        in_specs=[vmem] * 2,
        out_specs=[vmem] * 6,
        scratch_shapes=[
            pltpu.VMEM((2, rows, COL_HALO, channels), BF),
            pltpu.VMEM((2, rows, COL_HALO, channels), BF),
            pltpu.SemaphoreType.DMA((3 * len(DIRECTIONS),)),
            pltpu.SemaphoreType.DMA((3 * len(DIRECTIONS),)),
        ],
        compiler_params=pltpu.CompilerParams(
            collective_id=0, has_side_effects=True, vmem_limit_bytes=24 << 20
        ),
        name="halo",
    )(cells, cotangent)


def conv_kernel(
    cap, bins, grid_rows, grid_cols,
    tile_ref, valid_ref, h_ref, g_ref, h_ns, h_ew, h_corner, g_ns, g_ew, g_corner,
    weight_ref, cells_ref,
    out_ref, back_ref,
    fields, slopes, masks, wide_weight, grads, outer_grad, chosen,
):
    rows, cols = out_ref.shape[0], out_ref.shape[1]
    channels = out_ref.shape[2]
    width = cols + 2 * COL_HALO
    tall = rows + 2 * ROW_HALO
    row_first = lax.axis_index("cam") * rows - ROW_HALO
    col_first = lax.axis_index("tile") * cols - COL_HALO
    column = lax.broadcasted_iota(jnp.int32, (width, channels), 0) + col_first
    masks[0] = jnp.zeros((width, channels), F32)
    masks[1] = jnp.where((column >= 0) & (column < grid_cols), 1.0, 0.0)
    wide_weight[...] = jnp.zeros_like(wide_weight)

    def mask_of(row):
        at = row + row_first
        return masks[((at >= 0) & (at < grid_rows)).astype(jnp.int32)]

    def put(slot, row, value):
        fields[slot, row, :, 0:channels] = pltpu.roll(value, 1, 0).astype(BF)
        fields[slot, row, :, channels : 2 * channels] = value.astype(BF)
        fields[slot, row, :, 2 * channels : 3 * channels] = pltpu.roll(
            value, width - 1, 0
        ).astype(BF)

    def assemble(field, ns, ew, corner, halo, store):
        def pad(step, left, middle, right):
            row = step + ROW_HALO - halo
            whole = jnp.concatenate([left, middle, right], axis=0).astype(F32)
            store(step, row, jnp.where(mask_of(row) > 0.5, whole, 0.0))

        def upper(i, carry):
            pad(i, corner[0, i], ns[0, i], corner[1, i])
            return carry

        def inner(i, carry):
            pad(i + halo, ew[0, i], field[i], ew[1, i])
            return carry

        def lower(i, carry):
            pad(i + halo + rows, corner[2, i], ns[1, i], corner[3, i])
            return carry

        lax.fori_loop(0, halo, upper, 0)
        lax.fori_loop(0, rows, inner, 0)
        lax.fori_loop(0, halo, lower, 0)

    def keep_grad(step, row, value):
        outer_grad[step] = value.astype(BF)

    assemble(h_ref, h_ns, h_ew, h_corner, ROW_HALO, lambda step, row, value: put(0, row, value))
    assemble(g_ref, g_ns, g_ew, g_corner, LAYERS, keep_grad)

    def spread(index):
        slot = index % 2
        for j in range(2):
            for s in range(3):
                for r in range(3):
                    k = (r + j) * 3 + s
                    wide_weight[
                        slot, k * channels : (k + 1) * channels, j * channels : (j + 1) * channels
                    ] = weight_ref[index, r, s]

    def sweep(index, source, ranges):
        spread(index)
        for first, last, finish in ranges:
            def one(row, finish=finish):
                window = jnp.concatenate([fields[source, row - 1 + k] for k in range(4)], axis=1)
                both = jnp.dot(window, wide_weight[index % 2], preferred_element_type=F32)
                for j in range(2):
                    finish(row + j, both[:, j * channels : (j + 1) * channels])

            def two(step, carry, first=first, one=one):
                one(first + 4 * step)
                one(first + 4 * step + 2)
                return carry

            pairs = (last - first) // 2
            lax.fori_loop(0, pairs // 2, two, 0)
            if pairs % 2:
                one(last - 2)

    def activate(pre):
        sigma = 0.5 * jnp.tanh(0.5 * pre) + 0.5
        value = pre * sigma
        return value, sigma + value * (1.0 - sigma)

    for layer in range(1, LAYERS):
        def finish_forward(row, pre, layer=layer):
            value, slope = activate(pre)
            slopes[layer - 1, row] = slope
            put(layer % 2, row, value * mask_of(row))

        sweep(layer - 1, (layer - 1) % 2, [(layer, tall - layer, finish_forward)])

    def finish_last(row, pre):
        value, slope = activate(pre)
        grad = outer_grad[row - (ROW_HALO - LAYERS)].astype(F32)
        put(LAYERS % 2, row, grad * slope)
        return value

    def finish_own(row, pre):
        value = finish_last(row, pre)
        out_ref[row - ROW_HALO] = value[COL_HALO : COL_HALO + cols].astype(BF)

    sweep(
        LAYERS - 1, (LAYERS - 1) % 2,
        [
            (LAYERS, ROW_HALO, finish_last),
            (ROW_HALO, ROW_HALO + rows, finish_own),
            (ROW_HALO + rows, tall - LAYERS, finish_last),
        ],
    )

    for layer in range(LAYERS, 0, -1):
        done = LAYERS - layer

        def finish_backward(row, grad, layer=layer, done=done):
            grad = grad.astype(BF)
            if layer > 1:
                put(
                    (done + 1) % 2, row,
                    grad.astype(F32) * slopes[layer - 2, row] * mask_of(row),
                )
            else:
                inner = row - ROW_HALO
                for t in range(cols // TS):
                    grads[t, pl.ds(pl.multiple_of(inner * TS, TS), TS), :] = grad[
                        COL_HALO + t * TS : COL_HALO + (t + 1) * TS
                    ]

        sweep(
            LAYERS + layer - 1, done % 2,
            [(ROW_HALO + 1 - layer, ROW_HALO + rows - 1 + layer, finish_backward)],
        )

    slots = cells_ref.shape[1]
    lane = lax.broadcasted_iota(jnp.int32, (bins, slots), 1)
    cell = lax.broadcasted_iota(jnp.int32, (bins, TS * TS), 1).astype(F32)
    live_slots = list_slots(valid_ref, chosen)

    def send_back(step, carry):
        parts = []
        for k in range(GROUP):
            slot = chosen[jnp.minimum(step * GROUP + k, live_slots - 1)]
            place = jnp.sum(jnp.where(lane == slot, cells_ref[...], 0.0), axis=1, keepdims=True)
            hot = jnp.where(place == cell, 1.0, 0.0).astype(BF)
            parts.append(
                (slot, jnp.dot(hot, grads[tile_ref[slot]], preferred_element_type=F32))
            )
        for slot, part in parts:
            back_ref[pl.ds(pl.multiple_of(slot * bins, bins), bins), :] = part.astype(BF)
        return carry

    lax.fori_loop(0, (live_slots + GROUP - 1) // GROUP, send_back, 0)


def convolve(h, g, halos, weights, slot_tile, slot_valid, cells, cap, bins, grid_shape):
    rows, cols, channels = h.shape
    tall, wide = rows + 2 * ROW_HALO, cols + 2 * COL_HALO
    assert rows == TS
    vmem = pl.BlockSpec(memory_space=pltpu.VMEM)
    smem = pl.BlockSpec(memory_space=pltpu.SMEM)
    return pl.pallas_call(
        functools.partial(conv_kernel, cap, bins, *grid_shape),
        out_shape=[
            jax.ShapeDtypeStruct((rows, cols, channels), BF),
            jax.ShapeDtypeStruct((cells.shape[1] * bins, channels), BF),
        ],
        in_specs=[smem, smem] + [vmem] * 10,
        out_specs=[vmem, vmem],
        scratch_shapes=[
            pltpu.VMEM((2, tall, wide, 3 * channels), BF),
            pltpu.VMEM((LAYERS - 1, tall, wide, channels), F32),
            pltpu.VMEM((2, wide, channels), F32),
            pltpu.VMEM((2, 12 * channels, 2 * channels), BF),
            pltpu.VMEM((cols // TS, TS * TS, channels), BF),
            pltpu.VMEM((rows + 2 * LAYERS, wide, channels), BF),
            pltpu.SMEM((slot_valid.shape[0] + 1,), jnp.int32),
        ],
        compiler_params=pltpu.CompilerParams(vmem_limit_bytes=58 << 20),
        name="convolutions",
    )(slot_tile, slot_valid, h, g, *halos, weights, cells)


def final_kernel(slot_ref, depth_ref, context_ref, back_ref, grad_depth_ref, grad_context_ref):
    step = pl.program_id(0)
    blocks = depth_ref.shape[0]
    for b in range(blocks):
        rows = back_ref[slot_ref[step * blocks + b]]
        grad_context_ref[b] = lax.dot_general(
            depth_ref[b], rows, (((0,), (0,)), ((), ())), preferred_element_type=F32
        ).astype(BF)
        grad_depth_ref[b] = lax.dot_general(
            rows, context_ref[b], (((1,), (1,)), ((), ())), preferred_element_type=F32
        ).astype(BF)


def final(slot_index, depth, context, returned):
    blocks, bins, pixels = depth.shape
    channels = context.shape[2]
    chunk = 16
    depth_spec = pl.BlockSpec((chunk, bins, pixels), lambda i: (i, 0, 0))
    context_spec = pl.BlockSpec((chunk, pixels, channels), lambda i: (i, 0, 0))
    return pl.pallas_call(
        final_kernel,
        grid=(blocks // chunk,),
        out_shape=[
            jax.ShapeDtypeStruct(depth.shape, BF),
            jax.ShapeDtypeStruct(context.shape, BF),
        ],
        in_specs=[
            pl.BlockSpec(memory_space=pltpu.SMEM),
            depth_spec,
            context_spec,
            pl.BlockSpec(returned.shape, lambda i: (0, 0, 0)),
        ],
        out_specs=[depth_spec, context_spec],
        compiler_params=pltpu.CompilerParams(vmem_limit_bytes=40 << 20),
        name="final",
    )(slot_index, depth, context, returned)


def per_device(
    depth_weights, context, block_owner, block_local, block_cell, conv_weight, cotangent
):
    cams_here, blocks_cam, bins, pixels = depth_weights.shape
    channels = context.shape[3]
    rows, cols = cotangent.shape[0], cotangent.shape[1]
    cams = lax.axis_size("cam")
    tiles = lax.axis_size("tile")
    owners = cams * tiles
    blocks = cams_here * blocks_cam
    cap = max(2, 2 * blocks // owners)
    depth = depth_weights.reshape(blocks, bins, pixels)
    flat_context = context.reshape(blocks, pixels, channels)
    owner = block_owner.reshape(blocks)
    meta = jnp.concatenate(
        [
            block_cell.reshape(blocks, bins),
            block_local.reshape(blocks, 1),
            jnp.ones((blocks, 1), jnp.int32),
            jnp.zeros((blocks, 128 - bins - 2), jnp.int32),
        ],
        axis=1,
    ).astype(F32)
    sent = lift(depth, flat_context, owner, meta, owners, cap)
    received = lax.all_to_all(sent, ("cam", "tile"), split_axis=0, concat_axis=0, tiled=True)
    slot_meta = received[:, cap * bins : cap * bins + cap, :].reshape(owners * cap, 128)
    slot_tile = slot_meta[:, bins].astype(jnp.int32)
    slot_valid = slot_meta[:, bins + 1].astype(jnp.int32)
    wide_meta = slot_meta.astype(F32)
    slot_cells = wide_meta[:, :bins].T
    backward = jnp.swapaxes(conv_weight[:, ::-1, ::-1], 3, 4)
    weights = jnp.concatenate([conv_weight, backward], axis=0)
    cells = splat(received, slot_tile, slot_valid, wide_meta, cap, bins, rows, cols)
    halos = halo_exchange(cells, cotangent, cams, tiles)
    bev_out, back = convolve(
        cells, cotangent, halos, weights, slot_tile, slot_valid, slot_cells, cap, bins,
        (rows * cams, cols * tiles),
    )
    returned = lax.all_to_all(
        back.reshape(owners, cap * bins, channels),
        ("cam", "tile"), split_axis=0, concat_axis=0, tiled=True,
    ).reshape(owners * cap, bins, channels)
    positions = jnp.arange(blocks, dtype=jnp.int32)
    earlier = (owner[:, None] == owner[None, :]) & (positions[None, :] < positions[:, None])
    slot_index = owner * cap + jnp.sum(earlier.astype(jnp.int32), axis=1)
    grad_depth, grad_context = final(slot_index, depth, flat_context, returned)
    return (
        bev_out,
        grad_depth.reshape(depth_weights.shape),
        grad_context.reshape(context.shape),
    )


def solution(mesh):
    placed = (
        P(("cam", "tile"), None, None, None),
        P(("cam", "tile"), None, None, None),
        P(("cam", "tile"), None, None),
        P(("cam", "tile"), None),
        P(("cam", "tile"), None, None),
        P(),
        P("cam", "tile", None),
    )
    return jax.shard_map(
        per_device,
        mesh=mesh,
        in_specs=placed,
        out_specs=(
            P("cam", "tile", None),
            P(("cam", "tile"), None, None, None),
            P(("cam", "tile"), None, None, None),
        ),
        check_vma=False,
    )
```

```python
import functools

import jax
import jax.numpy as jnp
from jax import lax
from jax.experimental import pallas as pl
from jax.experimental.pallas import tpu as pltpu
from jax.sharding import PartitionSpec as P

TS = 16
LAYERS = 4
ROW_HALO = 2 * LAYERS
COL_HALO = 16
META_ROWS = 16
GROUP = 4
MESH = pl.DeviceIdType.MESH
BF = jnp.bfloat16
F32 = jnp.float32
DIRECTIONS = [(dx, dy) for dx in (-1, 0, 1) for dy in (-1, 0, 1) if (dx, dy) != (0, 0)]


def lift_kernel(cap, bins, owner_ref, meta_ref, depth_ref, context_ref, send_ref, count, meta_rows):
    step = pl.program_id(0)
    owners = send_ref.shape[0]
    blocks = depth_ref.shape[0]

    @pl.when(step == 0)
    def _():
        meta_rows[...] = jnp.zeros_like(meta_rows)

        def clear(o, carry):
            count[o] = 0
            return carry

        lax.fori_loop(0, owners, clear, 0)

    for b in range(blocks):
        owner = owner_ref[step * blocks + b]
        rank = count[owner]
        count[owner] = rank + 1
        lifted = jnp.dot(depth_ref[b], context_ref[b], preferred_element_type=F32).astype(BF)
        send_ref[owner, pl.ds(pl.multiple_of(rank * bins, bins), bins), :] = lifted
        meta_rows[owner, pl.ds(rank, 1), :] = meta_ref[pl.ds(b, 1), :]

    @pl.when(step == pl.num_programs(0) - 1)
    def _():
        def put(o, carry):
            rows = meta_rows[o]
            send_ref[o, cap * bins : cap * bins + META_ROWS, :] = jnp.concatenate(
                [rows, jnp.zeros_like(rows)], axis=0
            ).astype(BF)
            return carry

        lax.fori_loop(0, owners, put, 0)


def lift(depth, context, owner, meta, owners, cap):
    blocks, bins, pixels = depth.shape
    channels = context.shape[2]
    chunk = 16
    rows = cap * bins + META_ROWS
    return pl.pallas_call(
        functools.partial(lift_kernel, cap, bins),
        grid=(blocks // chunk,),
        out_shape=jax.ShapeDtypeStruct((owners, rows, channels), BF),
        in_specs=[
            pl.BlockSpec(memory_space=pltpu.SMEM),
            pl.BlockSpec((chunk, 128), lambda i: (i, 0)),
            pl.BlockSpec((chunk, bins, pixels), lambda i: (i, 0, 0)),
            pl.BlockSpec((chunk, pixels, channels), lambda i: (i, 0, 0)),
        ],
        out_specs=pl.BlockSpec((owners, rows, channels), lambda i: (0, 0, 0)),
        scratch_shapes=[pltpu.SMEM((owners,), jnp.int32), pltpu.VMEM((owners, 8, 128), F32)],
        compiler_params=pltpu.CompilerParams(vmem_limit_bytes=40 << 20),
        name="lift",
    )(owner, meta, depth, context)


def list_slots(valid_ref, chosen):
    def look(slot, count):
        chosen[count] = slot
        return count + valid_ref[slot]

    return lax.fori_loop(0, valid_ref.shape[0], look, 0)


def splat_kernel(cap, bins, tile_ref, valid_ref, meta_ref, recv_ref, out_ref, sums, chosen):
    tiles = sums.shape[0]
    cells = TS * TS
    sums[...] = jnp.zeros_like(sums)
    live_slots = list_slots(valid_ref, chosen)

    def group(step, carry):
        parts = []
        for k in range(GROUP):
            at = step * GROUP + k
            slot = chosen[jnp.minimum(at, live_slots - 1)]
            row = meta_ref[pl.ds(slot, 1), :][:, 0:bins]
            place = jnp.where(at < live_slots, row, -1.0)
            wide = jnp.broadcast_to(place, (cells, bins))
            index = lax.broadcasted_iota(jnp.int32, (cells, bins), 0).astype(F32)
            hot = jnp.where(wide == index, 1.0, 0.0).astype(BF)
            start = pl.multiple_of(slot % cap * bins, bins)
            rows = recv_ref[slot // cap, pl.ds(start, bins), :]
            parts.append((tile_ref[slot], jnp.dot(hot, rows, preferred_element_type=F32)))
        for tile, part in parts:
            sums[tile] = sums[tile] + part
        return carry

    lax.fori_loop(0, (live_slots + GROUP - 1) // GROUP, group, 0)
    for tile in range(tiles):
        for row in range(TS):
            out_ref[row, tile * TS : (tile + 1) * TS, :] = sums[
                tile, row * TS : (row + 1) * TS, :
            ].astype(BF)


def splat(received, slot_tile, slot_valid, slot_meta, cap, bins, rows, cols):
    channels = received.shape[2]
    tiles = (rows // TS) * (cols // TS)
    vmem = pl.BlockSpec(memory_space=pltpu.VMEM)
    smem = pl.BlockSpec(memory_space=pltpu.SMEM)
    return pl.pallas_call(
        functools.partial(splat_kernel, cap, bins),
        out_shape=jax.ShapeDtypeStruct((rows, cols, channels), BF),
        in_specs=[smem, smem, vmem, vmem],
        out_specs=vmem,
        scratch_shapes=[
            pltpu.VMEM((tiles, TS * TS, channels), F32),
            pltpu.SMEM((slot_valid.shape[0] + 1,), jnp.int32),
        ],
        compiler_params=pltpu.CompilerParams(vmem_limit_bytes=40 << 20),
        name="splat",
    )(slot_tile, slot_valid, slot_meta, received)


def halo_kernel(
    cams, tiles, h_ref, g_ref,
    h_ns, h_ew, h_corner, g_ns, g_ew, g_corner,
    h_edge, g_edge, send_sem, recv_sem,
):
    cam = lax.axis_index("cam")
    tile = lax.axis_index("tile")
    rows, cols = h_ref.shape[0], h_ref.shape[1]

    def there(dx, dy):
        ok = None
        for at, step, count in ((cam, dx, cams), (tile, dy, tiles)):
            if step:
                here = (at + step >= 0) & (at + step < count)
                ok = here if ok is None else ok & here
        return ok

    barrier = pltpu.get_barrier_semaphore()
    arrivals = 0
    for dx, dy in DIRECTIONS:
        near = there(dx, dy)
        arrivals = arrivals + near.astype(jnp.int32)

        @pl.when(near)
        def _():
            pl.semaphore_signal(
                barrier, inc=1, device_id=(cam + dx, tile + dy), device_id_type=MESH
            )

    for edge, field in ((h_edge, h_ref), (g_edge, g_ref)):
        edge[0] = field[:, 0:COL_HALO, :]
        edge[1] = field[:, cols - COL_HALO : cols, :]
    pl.semaphore_wait(barrier, arrivals)

    def copies(index):
        dx, dy = DIRECTIONS[index]
        side_row, side_col = (0 if dx == 1 else 1), (0 if dy == 1 else 1)
        own_col = 0 if dy == -1 else 1
        pairs = []
        for field, edge, ns, ew, corner, halo in (
            (h_ref, h_edge, h_ns, h_ew, h_corner, ROW_HALO),
            (g_ref, g_edge, g_ns, g_ew, g_corner, LAYERS),
        ):
            first = 0 if dx == -1 else rows - halo
            if dy == 0:
                for part in range(0, halo, LAYERS):
                    pairs.append(
                        (
                            field.at[pl.ds(first + part, LAYERS)],
                            ns.at[side_row, pl.ds(part, LAYERS)],
                        )
                    )
            elif dx == 0:
                pairs.append((edge.at[own_col], ew.at[side_col]))
            else:
                pairs.append(
                    (edge.at[own_col, pl.ds(first, halo)], corner.at[2 * side_row + side_col])
                )
        return [
            pltpu.make_async_remote_copy(
                src_ref=source,
                dst_ref=target,
                send_sem=send_sem.at[3 * index + which],
                recv_sem=recv_sem.at[3 * index + which],
                device_id=(cam + dx, tile + dy),
                device_id_type=MESH,
            )
            for which, (source, target) in enumerate(pairs)
        ]

    for index in range(len(DIRECTIONS)):
        @pl.when(there(*DIRECTIONS[index]))
        def _():
            for copy in copies(index):
                copy.start()

    for index, (dx, dy) in enumerate(DIRECTIONS):
        @pl.when(there(dx, dy))
        def _():
            for copy in copies(index):
                copy.wait_send()

        @pl.when(there(-dx, -dy))
        def _():
            for copy in copies(index):
                copy.wait_recv()


def halo_exchange(cells, cotangent, cams, tiles):
    rows, cols, channels = cells.shape
    vmem = pl.BlockSpec(memory_space=pltpu.VMEM)

    def parts(halo):
        return [
            jax.ShapeDtypeStruct((2, halo, cols, channels), BF),
            jax.ShapeDtypeStruct((2, rows, COL_HALO, channels), BF),
            jax.ShapeDtypeStruct((4, halo, COL_HALO, channels), BF),
        ]

    return pl.pallas_call(
        functools.partial(halo_kernel, cams, tiles),
        out_shape=parts(ROW_HALO) + parts(LAYERS),
        in_specs=[vmem] * 2,
        out_specs=[vmem] * 6,
        scratch_shapes=[
            pltpu.VMEM((2, rows, COL_HALO, channels), BF),
            pltpu.VMEM((2, rows, COL_HALO, channels), BF),
            pltpu.SemaphoreType.DMA((3 * len(DIRECTIONS),)),
            pltpu.SemaphoreType.DMA((3 * len(DIRECTIONS),)),
        ],
        compiler_params=pltpu.CompilerParams(
            collective_id=0, has_side_effects=True, vmem_limit_bytes=24 << 20
        ),
        name="halo",
    )(cells, cotangent)


def conv_kernel(
    cap, bins, grid_rows, grid_cols,
    tile_ref, valid_ref, h_ref, g_ref, h_ns_in, h_ew_in, h_corner_in, g_ns_in, g_ew_in,
    g_corner_in, weight_ref, cells_ref,
    out_ref, back_ref,
    fields, slopes, masks, wide_weight, grads, outer_grad, chosen,
    h_ns, h_ew, h_corner, g_ns, g_ew, g_corner, fetch_sem,
):
    fetches = [
        pltpu.make_async_copy(source, target, fetch_sem.at[which])
        for which, (source, target) in enumerate(
            (
                (h_ns_in, h_ns), (h_ew_in, h_ew), (h_corner_in, h_corner),
                (g_ns_in, g_ns), (g_ew_in, g_ew), (g_corner_in, g_corner),
            )
        )
    ]
    for fetch in fetches:
        fetch.start()
    rows, cols = out_ref.shape[0], out_ref.shape[1]
    channels = out_ref.shape[2]
    width = cols + 2 * COL_HALO
    tall = rows + 2 * ROW_HALO
    row_first = lax.axis_index("cam") * rows - ROW_HALO
    col_first = lax.axis_index("tile") * cols - COL_HALO
    column = lax.broadcasted_iota(jnp.int32, (width, channels), 0) + col_first
    masks[0] = jnp.zeros((width, channels), F32)
    masks[1] = jnp.where((column >= 0) & (column < grid_cols), 1.0, 0.0)
    wide_weight[...] = jnp.zeros_like(wide_weight)

    def mask_of(row):
        at = row + row_first
        return masks[((at >= 0) & (at < grid_rows)).astype(jnp.int32)]

    def put(slot, row, value):
        fields[slot, row, :, 0:channels] = pltpu.roll(value, 1, 0).astype(BF)
        fields[slot, row, :, channels : 2 * channels] = value.astype(BF)
        fields[slot, row, :, 2 * channels : 3 * channels] = pltpu.roll(
            value, width - 1, 0
        ).astype(BF)

    def assemble(field, ns, ew, corner, halo, store):
        def pad(step, left, middle, right):
            row = step + ROW_HALO - halo
            whole = jnp.concatenate([left, middle, right], axis=0).astype(F32)
            store(step, row, jnp.where(mask_of(row) > 0.5, whole, 0.0))

        def upper(i, carry):
            pad(i, corner[0, i], ns[0, i], corner[1, i])
            return carry

        def inner(i, carry):
            pad(i + halo, ew[0, i], field[i], ew[1, i])
            return carry

        def lower(i, carry):
            pad(i + halo + rows, corner[2, i], ns[1, i], corner[3, i])
            return carry

        lax.fori_loop(0, halo, upper, 0)
        lax.fori_loop(0, rows, inner, 0)
        lax.fori_loop(0, halo, lower, 0)

    for fetch in fetches:
        fetch.wait()

    def keep_grad(step, row, value):
        outer_grad[step] = value.astype(BF)

    assemble(h_ref, h_ns, h_ew, h_corner, ROW_HALO, lambda step, row, value: put(0, row, value))
    assemble(g_ref, g_ns, g_ew, g_corner, LAYERS, keep_grad)

    def spread(index):
        slot = index % 2
        for j in range(2):
            for s in range(3):
                for r in range(3):
                    k = (r + j) * 3 + s
                    wide_weight[
                        slot, k * channels : (k + 1) * channels, j * channels : (j + 1) * channels
                    ] = weight_ref[index, r, s]

    def sweep(index, source, ranges):
        spread(index)
        for first, last, finish in ranges:
            def some(row, count, finish=finish):
                window = jnp.concatenate(
                    [
                        jnp.concatenate(
                            [fields[source, row - 1 + k + 2 * pair] for pair in range(count)],
                            axis=0,
                        )
                        for k in range(4)
                    ],
                    axis=1,
                )
                both = jnp.dot(window, wide_weight[index % 2], preferred_element_type=F32)
                for pair in range(count):
                    for j in range(2):
                        finish(
                            row + 2 * pair + j,
                            both[
                                pair * width : (pair + 1) * width,
                                j * channels : (j + 1) * channels,
                            ],
                        )

            def step_of(step, carry, first=first, some=some):
                some(first + 4 * step, 2)
                return carry

            pairs = (last - first) // 2
            lax.fori_loop(0, pairs // 2, step_of, 0)
            if pairs % 2:
                some(last - 2, 1)

    def activate(pre):
        sigma = 0.5 * jnp.tanh(0.5 * pre) + 0.5
        value = pre * sigma
        return value, sigma + value * (1.0 - sigma)

    for layer in range(1, LAYERS):
        def finish_forward(row, pre, layer=layer):
            value, slope = activate(pre)
            slopes[layer - 1, row] = slope
            put(layer % 2, row, value * mask_of(row))

        sweep(layer - 1, (layer - 1) % 2, [(layer, tall - layer, finish_forward)])

    def finish_last(row, pre):
        value, slope = activate(pre)
        grad = outer_grad[row - (ROW_HALO - LAYERS)].astype(F32)
        put(LAYERS % 2, row, grad * slope)
        return value

    def finish_own(row, pre):
        value = finish_last(row, pre)
        out_ref[row - ROW_HALO] = value[COL_HALO : COL_HALO + cols].astype(BF)

    sweep(
        LAYERS - 1, (LAYERS - 1) % 2,
        [
            (LAYERS, ROW_HALO, finish_last),
            (ROW_HALO, ROW_HALO + rows, finish_own),
            (ROW_HALO + rows, tall - LAYERS, finish_last),
        ],
    )

    for layer in range(LAYERS, 0, -1):
        done = LAYERS - layer

        def finish_backward(row, grad, layer=layer, done=done):
            grad = grad.astype(BF)
            if layer > 1:
                put(
                    (done + 1) % 2, row,
                    grad.astype(F32) * slopes[layer - 2, row] * mask_of(row),
                )
            else:
                inner = row - ROW_HALO
                for t in range(cols // TS):
                    grads[t, pl.ds(pl.multiple_of(inner * TS, TS), TS), :] = grad[
                        COL_HALO + t * TS : COL_HALO + (t + 1) * TS
                    ]

        sweep(
            LAYERS + layer - 1, done % 2,
            [(ROW_HALO + 1 - layer, ROW_HALO + rows - 1 + layer, finish_backward)],
        )

    slots = cells_ref.shape[1]
    lane = lax.broadcasted_iota(jnp.int32, (bins, slots), 1)
    cell = lax.broadcasted_iota(jnp.int32, (bins, TS * TS), 1).astype(F32)
    live_slots = list_slots(valid_ref, chosen)

    def send_back(step, carry):
        parts = []
        for k in range(GROUP):
            slot = chosen[jnp.minimum(step * GROUP + k, live_slots - 1)]
            place = jnp.sum(jnp.where(lane == slot, cells_ref[...], 0.0), axis=1, keepdims=True)
            hot = jnp.where(place == cell, 1.0, 0.0).astype(BF)
            parts.append(
                (slot, jnp.dot(hot, grads[tile_ref[slot]], preferred_element_type=F32))
            )
        for slot, part in parts:
            back_ref[pl.ds(pl.multiple_of(slot * bins, bins), bins), :] = part.astype(BF)
        return carry

    lax.fori_loop(0, (live_slots + GROUP - 1) // GROUP, send_back, 0)


def convolve(h, g, halos, weights, slot_tile, slot_valid, cells, cap, bins, grid_shape):
    rows, cols, channels = h.shape
    tall, wide = rows + 2 * ROW_HALO, cols + 2 * COL_HALO
    assert rows == TS
    vmem = pl.BlockSpec(memory_space=pltpu.VMEM)
    smem = pl.BlockSpec(memory_space=pltpu.SMEM)
    return pl.pallas_call(
        functools.partial(conv_kernel, cap, bins, *grid_shape),
        out_shape=[
            jax.ShapeDtypeStruct((rows, cols, channels), BF),
            jax.ShapeDtypeStruct((cells.shape[1] * bins, channels), BF),
        ],
        in_specs=[smem, smem, vmem, vmem] + [pl.BlockSpec(memory_space=pl.ANY)] * 6 + [vmem] * 2,
        out_specs=[vmem, vmem],
        scratch_shapes=[
            pltpu.VMEM((2, tall, wide, 3 * channels), BF),
            pltpu.VMEM((LAYERS - 1, tall, wide, channels), F32),
            pltpu.VMEM((2, wide, channels), F32),
            pltpu.VMEM((2, 12 * channels, 2 * channels), BF),
            pltpu.VMEM((cols // TS, TS * TS, channels), BF),
            pltpu.VMEM((rows + 2 * LAYERS, wide, channels), BF),
            pltpu.SMEM((slot_valid.shape[0] + 1,), jnp.int32),
        ]
        + [pltpu.VMEM(part.shape, BF) for part in halos]
        + [pltpu.SemaphoreType.DMA((len(halos),))],
        compiler_params=pltpu.CompilerParams(vmem_limit_bytes=58 << 20),
        name="convolutions",
    )(slot_tile, slot_valid, h, g, *halos, weights, cells)


def final_kernel(slot_ref, depth_ref, context_ref, back_ref, grad_depth_ref, grad_context_ref):
    step = pl.program_id(0)
    blocks = depth_ref.shape[0]
    for b in range(blocks):
        rows = back_ref[slot_ref[step * blocks + b]]
        grad_context_ref[b] = lax.dot_general(
            depth_ref[b], rows, (((0,), (0,)), ((), ())), preferred_element_type=F32
        ).astype(BF)
        grad_depth_ref[b] = lax.dot_general(
            rows, context_ref[b], (((1,), (1,)), ((), ())), preferred_element_type=F32
        ).astype(BF)


def final(slot_index, depth, context, returned):
    blocks, bins, pixels = depth.shape
    channels = context.shape[2]
    chunk = 16
    depth_spec = pl.BlockSpec((chunk, bins, pixels), lambda i: (i, 0, 0))
    context_spec = pl.BlockSpec((chunk, pixels, channels), lambda i: (i, 0, 0))
    return pl.pallas_call(
        final_kernel,
        grid=(blocks // chunk,),
        out_shape=[
            jax.ShapeDtypeStruct(depth.shape, BF),
            jax.ShapeDtypeStruct(context.shape, BF),
        ],
        in_specs=[
            pl.BlockSpec(memory_space=pltpu.SMEM),
            depth_spec,
            context_spec,
            pl.BlockSpec(returned.shape, lambda i: (0, 0, 0)),
        ],
        out_specs=[depth_spec, context_spec],
        compiler_params=pltpu.CompilerParams(vmem_limit_bytes=40 << 20),
        name="final",
    )(slot_index, depth, context, returned)


def per_device(
    depth_weights, context, block_owner, block_local, block_cell, conv_weight, cotangent
):
    cams_here, blocks_cam, bins, pixels = depth_weights.shape
    channels = context.shape[3]
    rows, cols = cotangent.shape[0], cotangent.shape[1]
    cams = lax.axis_size("cam")
    tiles = lax.axis_size("tile")
    owners = cams * tiles
    blocks = cams_here * blocks_cam
    cap = max(2, 2 * blocks // owners)
    depth = depth_weights.reshape(blocks, bins, pixels)
    flat_context = context.reshape(blocks, pixels, channels)
    owner = block_owner.reshape(blocks)
    meta = jnp.concatenate(
        [
            block_cell.reshape(blocks, bins),
            block_local.reshape(blocks, 1),
            jnp.ones((blocks, 1), jnp.int32),
            jnp.zeros((blocks, 128 - bins - 2), jnp.int32),
        ],
        axis=1,
    ).astype(F32)
    sent = lift(depth, flat_context, owner, meta, owners, cap)
    received = lax.all_to_all(sent, ("cam", "tile"), split_axis=0, concat_axis=0, tiled=True)
    slot_meta = received[:, cap * bins : cap * bins + cap, :].reshape(owners * cap, 128)
    slot_tile = slot_meta[:, bins].astype(jnp.int32)
    slot_valid = slot_meta[:, bins + 1].astype(jnp.int32)
    wide_meta = slot_meta.astype(F32)
    slot_cells = wide_meta[:, :bins].T
    backward = jnp.swapaxes(conv_weight[:, ::-1, ::-1], 3, 4)
    weights = jnp.concatenate([conv_weight, backward], axis=0)
    cells = splat(received, slot_tile, slot_valid, wide_meta, cap, bins, rows, cols)
    halos = halo_exchange(cells, cotangent, cams, tiles)
    bev_out, back = convolve(
        cells, cotangent, halos, weights, slot_tile, slot_valid, slot_cells, cap, bins,
        (rows * cams, cols * tiles),
    )
    returned = lax.all_to_all(
        back.reshape(owners, cap * bins, channels),
        ("cam", "tile"), split_axis=0, concat_axis=0, tiled=True,
    ).reshape(owners * cap, bins, channels)
    positions = jnp.arange(blocks, dtype=jnp.int32)
    earlier = (owner[:, None] == owner[None, :]) & (positions[None, :] < positions[:, None])
    slot_index = owner * cap + jnp.sum(earlier.astype(jnp.int32), axis=1)
    grad_depth, grad_context = final(slot_index, depth, flat_context, returned)
    return (
        bev_out,
        grad_depth.reshape(depth_weights.shape),
        grad_context.reshape(context.shape),
    )


def solution(mesh):
    placed = (
        P(("cam", "tile"), None, None, None),
        P(("cam", "tile"), None, None, None),
        P(("cam", "tile"), None, None),
        P(("cam", "tile"), None),
        P(("cam", "tile"), None, None),
        P(),
        P("cam", "tile", None),
    )
    return jax.shard_map(
        per_device,
        mesh=mesh,
        in_specs=placed,
        out_specs=(
            P("cam", "tile", None),
            P(("cam", "tile"), None, None, None),
            P(("cam", "tile"), None, None, None),
        ),
        check_vma=False,
    )
```
